1024 devices in a mesh: rep: 8 (over x_hi, core), shard: 128 (over z, x_lo, y).
Axes of the slice: x: 8 (x_hi: 4, x_lo: 2; x = x_hi * 2 + x_lo), y: 8, z: 8, core: 2. Of those that a mesh axis runs over, the one named last changes fastest.
Arguments:
- latents: bfloat16 [1024, 24, 20, 384], P(('rep', 'shard')), may hold values from -6 to 6
- norm_gain: float32 [384], replicated, may hold values from 0.1 to 1.9
- norm_bias: float32 [384], replicated, may hold values from -3 to 3
- conv_weight: bfloat16 [3, 1152, 384], P(None, 'shard'), may hold values from -0.109375 to 0.109375
- cotangent: bfloat16 [1024, 24, 20, 384], P(('rep', 'shard')), may hold values from -6 to 6
Outputs:
- output: bfloat16 [1024, 24, 20, 384], P(('rep', 'shard'))
- grad_input: bfloat16 [1024, 24, 20, 384], P(('rep', 'shard'))
- grad_weight: float32 [3, 1152, 384], P(None, 'shard')
The draws below stay inside these ranges and needn't reach their ends.
All inputs are finite; a program needn't handle non-finite values.
Results may differ from the reference program's by a relative error of at most 0.0035.
Values may be sent and summed in bfloat16 or wider, within the bound.
No kernel may reach another device: no remote copies, remote signals or barrier semaphores. Data moves between devices by JAX's collectives and lax.ppermute only.
A program may use at most 128 MiB of HBM per device.

```python
import jax
import jax.numpy as jnp
from jax import lax

C = 384
GROUPS = 32
HEIGHT = 24
WIDTH = 20
BATCH = 1024
TAPROWS = 1152


def steps_of(own_key, dims, shards, least, high):
    def one(axis_at, shards_of):
        draws = jax.random.uniform(jax.random.fold_in(jax.random.fold_in(own_key, 6), axis_at), (shards_of,), jnp.float32, least / len(shards), high / len(shards))
        return jnp.repeat(jnp.exp(draws), dims[axis_at] // shards_of).reshape((-1,) + (1,) * (len(dims) - axis_at - 1))

    gain = one(*shards[0])
    for cut in shards[1:]:
        gain = gain * one(*cut)
    return gain


def scatter_about(rng, extent, scale, most, pieces=(), dtype=jnp.bfloat16):
    drawn = jax.random.normal(rng, extent, jnp.float32) * scale
    if len(pieces) > 0:
        drawn = steps_of(rng, extent, pieces, -0.22, 0.18) * drawn
    return jnp.clip(drawn, min=-most, max=most).astype(dtype)


def setup_inputs(seed: int = 0) -> dict:
    keys = jax.random.split(jax.random.key(seed), 6)
    latents = scatter_about(keys[0], (BATCH, HEIGHT, WIDTH, C), 1.0, 6.0, ((0, 1024),))
    norm_gain = jnp.clip(1.0 + 0.18 * jax.random.normal(keys[1], (C,), jnp.float32), 0.1, 1.9)
    norm_bias = scatter_about(keys[2], (C,), 0.5, 3.0, (), jnp.float32)
    conv_weight = scatter_about(keys[3], (3, TAPROWS, C), (3 * TAPROWS) ** -0.5, 0.109375, ((1, 128),))
    cotangent = scatter_about(keys[4], (BATCH, HEIGHT, WIDTH, C), 1.0, 6.0, ((0, 1024),))
    return dict(latents=latents, norm_gain=norm_gain, norm_bias=norm_bias, conv_weight=conv_weight, cotangent=cotangent)


def norm_act(values, norm_gain, norm_bias):
    shape = values.shape
    per = shape[-1] // GROUPS
    grouped = values.reshape(shape[:-1] + (GROUPS, per))
    mean = lax.optimization_barrier(jnp.mean(grouped, axis=(1, 2, 4), keepdims=True))
    centred = grouped - mean
    variance = lax.optimization_barrier(jnp.mean(centred * centred, axis=(1, 2, 4), keepdims=True))
    normed = (centred / jnp.sqrt(variance + 1e-05)).reshape(shape) * norm_gain + norm_bias
    return jax.nn.silu(normed)

def row_patches(activated, kernel_row):
    count, rows, cols, chans = activated.shape
    padded = jnp.pad(activated, ((0, 0), (1, 1), (1, 1), (0, 0)))
    taps = [padded[:, kernel_row:kernel_row + rows, j:j + cols, :] for j in range(3)]
    return jnp.concatenate(taps, axis=-1).reshape(count * rows * cols, chans * 3)

def reference(latents, norm_gain, norm_bias, conv_weight, cotangent):

    def one_latent(carry, pair):
        sample, upstream = pair
        sample = sample[None]
        upstream = upstream[None]
        values = sample.astype(jnp.float32)
        activated = norm_act(values, norm_gain, norm_bias).astype(jnp.bfloat16)
        flat_up = upstream.reshape(HEIGHT * WIDTH, C)
        pre = jnp.zeros((HEIGHT * WIDTH, C), jnp.float32)
        total = jnp.zeros((1, HEIGHT + 2, WIDTH + 2, C), jnp.float32)
        blocks = []
        for i in range(3):
            patches = row_patches(activated, i)
            pre = pre + jnp.dot(patches, conv_weight[i], preferred_element_type=jnp.float32)
            patch_grad = jnp.dot(flat_up, conv_weight[i].T, preferred_element_type=jnp.float32)
            parts = patch_grad.reshape(1, HEIGHT, WIDTH, 3, C)
            for j in range(3):
                total = total + jnp.pad(parts[:, :, :, j, :], ((0, 0), (i, 2 - i), (j, 2 - j), (0, 0)))
            blocks.append(jnp.dot(patches.T, flat_up, preferred_element_type=jnp.float32))
        result = (values + pre.reshape(values.shape)).astype(jnp.bfloat16)
        act_grad = total[:, 1:-1, 1:-1, :]
        unused, pullback = jax.vjp(lambda v: norm_act(v, norm_gain, norm_bias), values)
        back = pullback(act_grad)[0]
        grad_in = (upstream.astype(jnp.float32) + back).astype(jnp.bfloat16)
        carry = carry + jnp.stack(blocks)
        return (carry, (result[0], grad_in[0]))
    start = jnp.zeros((3, TAPROWS, C), jnp.float32)
    total, outs = lax.scan(one_latent, start, (latents, cotangent))
    return (outs[0], outs[1], total / BATCH)
```

```python
import jax
import jax.numpy as jnp
from jax import lax
from jax.sharding import Mesh
from jax.sharding import PartitionSpec as P

GROUPS = 32
AXES = ("xh", "core", "z", "xl", "y")
SWAP = ((0, 0), (1, 2), (2, 1), (3, 3))


def norm_act(values, norm_gain, norm_bias):
    shape = values.shape
    per = shape[-1] // GROUPS
    grouped = values.reshape(shape[:-1] + (GROUPS, per))
    mean = jnp.mean(grouped, axis=(1, 2, 4), keepdims=True)
    centred = grouped - mean
    variance = jnp.mean(centred * centred, axis=(1, 2, 4), keepdims=True)
    normed = (centred / jnp.sqrt(variance + 1e-05)).reshape(shape) * norm_gain + norm_bias
    return jax.nn.silu(normed)


def spread(block, axis):
    count = lax.axis_size(axis)
    copies = jnp.broadcast_to(block[None], (count,) + block.shape)
    return lax.all_to_all(copies, axis, 0, 0, tiled=True)


def gather_weight(conv_weight, core):
    taps, rows, chans = conv_weight.shape
    block = lax.ppermute(conv_weight.reshape(taps * rows, chans), ("core", "xl"), SWAP)
    block = spread(block, "z")
    block = spread(block, "y")
    other = lax.ppermute(block, "core", ((0, 1), (1, 0)))
    low = jnp.where(core == 0, block, other)
    high = jnp.where(core == 0, other, block)
    full = jnp.stack([low, high])
    ys, zs = full.shape[1:3]
    full = full.reshape(2, ys, zs, taps, rows, chans).transpose(3, 2, 0, 1, 4, 5)
    return full.reshape(taps, zs * 2 * ys * rows, chans)


def reduce_terms(terms, core):
    taps, total, chans = terms.shape
    ys, zs = lax.axis_size("y"), lax.axis_size("z")
    rows = total // (2 * ys * zs)
    parts = terms.reshape(taps, zs, 2, ys, rows, chans).transpose(2, 3, 1, 0, 4, 5)
    parts = parts.reshape(2, ys, zs, taps * rows, chans)
    keep = jnp.where(core == 0, parts[0], parts[1])
    send = jnp.where(core == 0, parts[1], parts[0]).astype(jnp.bfloat16)
    got = lax.ppermute(send, "core", ((0, 1), (1, 0)))
    own = (keep + got.astype(jnp.float32)).astype(jnp.bfloat16)
    own = lax.all_to_all(own, "y", 0, 0, tiled=True).astype(jnp.float32).sum(0)
    own = lax.all_to_all(own.astype(jnp.bfloat16), "z", 0, 0, tiled=True)
    own = own.astype(jnp.float32).sum(0)
    own = spread(own, ("xh", "xl")).sum(0)
    return lax.ppermute(own, ("core", "xl"), SWAP).reshape(taps, rows, chans)


def body(latents, norm_gain, norm_bias, conv_weight, cotangent):
    count, rows, cols, chans = latents.shape
    scale = 1.0 / (count * lax.axis_size(AXES))
    core = lax.axis_index("core")
    cells = count * rows * cols
    weight_full = gather_weight(conv_weight, core)
    values = latents.astype(jnp.float32)
    activated = norm_act(values, norm_gain, norm_bias).astype(jnp.bfloat16)
    padded = jnp.pad(activated, ((0, 0), (1, 1), (1, 1), (0, 0)))
    flat_up = cotangent.reshape(cells, chans)
    pre = jnp.zeros((cells, chans), jnp.float32)
    total = jnp.zeros((count, rows + 2, cols + 2, chans), jnp.float32)
    patch_rows = []
    for i in range(3):
        taps = [padded[:, i : i + rows, j : j + cols, :] for j in range(3)]
        patches = jnp.concatenate(taps, axis=-1).reshape(cells, 3 * chans)
        patch_rows.append(patches)
    terms = jnp.stack(
        [jnp.einsum("pk,pc->kc", p, flat_up, preferred_element_type=jnp.float32) for p in patch_rows]
    )
    grad_weight = reduce_terms(terms, core) * scale
    for i in range(3):
        pre = pre + jnp.dot(patch_rows[i], weight_full[i], preferred_element_type=jnp.float32)
        patch_grad = jnp.einsum(
            "pc,kc->pk", flat_up, weight_full[i], preferred_element_type=jnp.float32
        )
        parts = patch_grad.reshape(count, rows, cols, 3, chans)
        for j in range(3):
            total = total + jnp.pad(parts[:, :, :, j, :], ((0, 0), (i, 2 - i), (j, 2 - j), (0, 0)))
    output = (values + pre.reshape(values.shape)).astype(jnp.bfloat16)
    act_grad = total[:, 1:-1, 1:-1, :]
    unused, pullback = jax.vjp(lambda v: norm_act(v, norm_gain, norm_bias), values)
    back = pullback(act_grad)[0]
    grad_input = (cotangent.astype(jnp.float32) + back).astype(jnp.bfloat16)
    return (output, grad_input, grad_weight)


def solution(mesh):
    fine = Mesh(mesh.devices.reshape(4, 2, 8, 2, 8), AXES)
    batch = P(("xh", "core", "z", "xl", "y"), None, None, None)
    weight = P(None, ("z", "xl", "y"), None)
    return jax.shard_map(
        body,
        mesh=fine,
        in_specs=(batch, P(), P(), weight, batch),
        out_specs=(batch, batch, weight),
        check_vma=False,
    )
```

```python
import functools

import jax
import jax.numpy as jnp
import numpy as np
from jax import lax
from jax.experimental import pallas as pl
from jax.experimental.pallas import tpu as pltpu
from jax.sharding import Mesh
from jax.sharding import PartitionSpec as P

GROUPS = 32
HEIGHT, WIDTH, CHANS = 24, 20, 384
CELLS = HEIGHT * WIDTH
PER = CHANS // GROUPS
TOP = 24
ROWS = 9
YS, ZS = 8, 8
PACK = 224
ZROWS = 2 * YS * ROWS
AXES = ("xh", "core", "z", "xl", "y")
SWAP = ((0, 0), (1, 2), (2, 1), (3, 3))
VMEM_LIMIT = 40 * 1024 * 1024


def placement():
    sel = np.zeros((2, PACK, 3 * ZROWS), np.float32)
    for half in range(2):
        for y in range(YS):
            for i in range(3):
                for r in range(ROWS):
                    row = (half * YS + y) * ROWS + r
                    sel[half, (y * 3 + i) * ROWS + r, i * ZROWS + row] = 1.0
    return sel


SEL = placement()


def dot(a, b, dims=((1,), (0,))):
    return lax.dot_general(a, b, (dims, ((), ())), preferred_element_type=jnp.float32)


def group_mean(row):
    a = lax.broadcasted_iota(jnp.int32, (CHANS, GROUPS), 0)
    b = lax.broadcasted_iota(jnp.int32, (CHANS, GROUPS), 1) * PER
    member = jnp.where((a >= b) & (a < b + PER), 1.0, 0.0).astype(jnp.float32)
    total = lax.dot_general(
        row, member, (((1,), (0,)), ((), ())),
        precision=lax.Precision.HIGHEST, preferred_element_type=jnp.float32,
    )
    back = lax.dot_general(
        total, member, (((1,), (1,)), ((), ())),
        precision=lax.Precision.HIGHEST, preferred_element_type=jnp.float32,
    )
    return back * (1.0 / (CELLS * PER))


def channel_sum(values):
    return jnp.broadcast_to(jnp.sum(values, axis=0, keepdims=True), (8, CHANS))


def flatten(ref, flat):
    for h in range(HEIGHT):
        flat[h * WIDTH : (h + 1) * WIDTH, :] = ref[0, h].astype(jnp.float32)


def statistics(flat):
    mean = group_mean(channel_sum(flat[...]))[0:1]
    centred = flat[...] - mean
    variance = group_mean(channel_sum(centred * centred))[0:1]
    return mean, 1.0 / jnp.sqrt(variance + 1e-05)


def build_patches(shifted, patches):
    col = lax.broadcasted_iota(jnp.int32, (CELLS, CHANS), 0) % WIDTH
    for i in range(3):
        for j in range(3):
            start = TOP + (i - 1) * WIDTH + (j - 1)
            tap = shifted[start : start + CELLS, :]
            if j == 0:
                tap = jnp.where(col == 0, 0.0, tap)
            if j == 2:
                tap = jnp.where(col == WIDTH - 1, 0.0, tap)
            at = (i * 3 + j) * CHANS
            patches[:, at : at + CHANS] = tap.astype(jnp.bfloat16)


def clear_edges(shifted):
    edge = jnp.zeros((TOP, CHANS), jnp.float32)
    shifted[:TOP, :] = edge
    shifted[TOP + CELLS :, :] = edge


def activate(flat, gain, bias, shifted):
    mean, inverse = statistics(flat)
    normed = (flat[...] - mean) * inverse * gain[...] + bias[...]
    active = normed / (1.0 + jnp.exp(-normed))
    shifted[TOP : TOP + CELLS, :] = active.astype(jnp.bfloat16).astype(jnp.float32)
    return mean, inverse


def term_kernel(core, lat, gain, bias, cot, sel, keep, send, flat, shifted, up, patches, terms):
    clear_edges(shifted)
    flatten(cot, flat)
    up[...] = flat[...].astype(jnp.bfloat16)
    flatten(lat, flat)
    activate(flat, gain, bias, shifted)
    build_patches(shifted, patches)
    for t in range(9):
        at = t * CHANS
        terms[at : at + CHANS, :] = dot(patches[:, at : at + CHANS], up[...], ((0,), (0,)))
    mine, other = sel[core[0]], sel[1 - core[0]]
    for z in range(ZS):
        block = jnp.concatenate(
            [terms[i * 3 * CHANS + z * ZROWS : i * 3 * CHANS + (z + 1) * ZROWS, :] for i in range(3)]
        )
        high = block.astype(jnp.bfloat16)
        low = (block - high.astype(jnp.float32)).astype(jnp.bfloat16)
        keep[z] = dot(mine, high) + dot(mine, low)
        send[z] = dot(other, high).astype(jnp.bfloat16)


def layer_kernel(
    core, lat, gain, bias, cot, held, got, sel, out, grad, flat, shifted, up, patches, weight
):
    clear_edges(shifted)
    flatten(cot, up)
    flatten(lat, flat)
    mean, inverse = activate(flat, gain, bias, shifted)
    build_patches(shifted, patches)
    mine, other = sel[core[0]], sel[1 - core[0]]
    for z in range(ZS):
        block = dot(mine, held[z], ((0,), (0,))) + dot(other, got[z], ((0,), (0,)))
        for i in range(3):
            at = i * 3 * CHANS + z * ZROWS
            weight[at : at + ZROWS, :] = block[i * ZROWS : (i + 1) * ZROWS].astype(jnp.bfloat16)
    result = dot(patches[...], weight[...]) + flat[...]
    shifted[TOP : TOP + CELLS, :] = up[...]
    for h in range(HEIGHT):
        out[0, h] = result[h * WIDTH : (h + 1) * WIDTH].astype(jnp.bfloat16)
    build_patches(shifted, patches)
    back = jnp.zeros((CELLS, CHANS), jnp.float32)
    for t in range(9):
        at, mirror = t * CHANS, (8 - t) * CHANS
        back = back + dot(
            patches[:, mirror : mirror + CHANS], weight[at : at + CHANS, :], ((1,), (1,))
        )
    hat = (flat[...] - mean) * inverse
    normed = hat * gain[...] + bias[...]
    gate = 1.0 / (1.0 + jnp.exp(-normed))
    back = back * (gate * (1.0 + normed * (1.0 - gate))) * gain[...]
    first = group_mean(channel_sum(back))[0:1]
    second = group_mean(channel_sum(back * hat))[0:1]
    result = up[...] + inverse * (back - first - hat * second)
    for h in range(HEIGHT):
        grad[0, h] = result[h * WIDTH : (h + 1) * WIDTH].astype(jnp.bfloat16)


VMEM = functools.partial(pl.BlockSpec, memory_space=pltpu.VMEM)
SMEM = functools.partial(pl.BlockSpec, memory_space=pltpu.SMEM)


def spread(block, axis):
    count = lax.axis_size(axis)
    copies = jnp.broadcast_to(block[None], (count,) + block.shape)
    return lax.all_to_all(copies, axis, 0, 0, tiled=True)


def gather_halves(conv_weight):
    taps, rows, chans = conv_weight.shape
    block = lax.ppermute(conv_weight.reshape(taps * rows, chans), ("core", "xl"), SWAP)
    block = spread(block, "y").reshape(YS * taps * rows, chans)
    block = jnp.pad(block, ((0, PACK - YS * taps * rows), (0, 0)))
    held = spread(block, "z")
    return held, lax.ppermute(held, "core", ((0, 1), (1, 0)))


def reduce_terms(keep, send):
    got = lax.ppermute(send, "core", ((0, 1), (1, 0)))
    own = (keep + got.astype(jnp.float32)).astype(jnp.bfloat16)
    own = lax.all_to_all(own, "z", 0, 0, tiled=True).astype(jnp.float32).sum(0)
    own = own[: YS * 3 * ROWS].reshape(YS, 3 * ROWS, CHANS).astype(jnp.bfloat16)
    own = lax.all_to_all(own, "y", 0, 0, tiled=True).astype(jnp.float32).sum(0)
    own = spread(own, ("xh", "xl")).sum(0)
    return lax.ppermute(own, ("core", "xl"), SWAP).reshape(3, ROWS, CHANS)


def terms_of(core, latents, gain, bias, cotangent, sel, **options):
    packed = (ZS, PACK, CHANS)
    return pl.pallas_call(
        term_kernel,
        out_shape=(
            jax.ShapeDtypeStruct(packed, jnp.float32),
            jax.ShapeDtypeStruct(packed, jnp.bfloat16),
        ),
        in_specs=[SMEM()] + [VMEM()] * 5,
        out_specs=(VMEM(), VMEM()),
        scratch_shapes=[
            pltpu.VMEM((CELLS, CHANS), jnp.float32),
            pltpu.VMEM((CELLS + 2 * TOP, CHANS), jnp.float32),
            pltpu.VMEM((CELLS, CHANS), jnp.bfloat16),
            pltpu.VMEM((CELLS, 9 * CHANS), jnp.bfloat16),
            pltpu.VMEM((9 * CHANS, CHANS), jnp.float32),
        ],
        compiler_params=pltpu.CompilerParams(vmem_limit_bytes=VMEM_LIMIT),
        cost_estimate=pl.CostEstimate(
            flops=4 * 10**9, bytes_accessed=8 * 10**6, transcendentals=CELLS * CHANS
        ),
        **options,
    )(core, latents, gain, bias, cotangent, sel)


def layer_of(core, latents, gain, bias, cotangent, held, got, sel, **options):
    return pl.pallas_call(
        layer_kernel,
        out_shape=(
            jax.ShapeDtypeStruct(latents.shape, jnp.bfloat16),
            jax.ShapeDtypeStruct(latents.shape, jnp.bfloat16),
        ),
        in_specs=[SMEM()] + [VMEM()] * 7,
        out_specs=(VMEM(), VMEM()),
        scratch_shapes=[
            pltpu.VMEM((CELLS, CHANS), jnp.float32),
            pltpu.VMEM((CELLS + 2 * TOP, CHANS), jnp.float32),
            pltpu.VMEM((CELLS, CHANS), jnp.float32),
            pltpu.VMEM((CELLS, 9 * CHANS), jnp.bfloat16),
            pltpu.VMEM((9 * CHANS, CHANS), jnp.bfloat16),
        ],
        compiler_params=pltpu.CompilerParams(vmem_limit_bytes=VMEM_LIMIT),
        cost_estimate=pl.CostEstimate(
            flops=4 * 10**9, bytes_accessed=8 * 10**6, transcendentals=2 * CELLS * CHANS
        ),
        **options,
    )(core, latents, gain, bias, cotangent, held, got, sel)


def body(latents, norm_gain, norm_bias, conv_weight, cotangent):
    scale = 1.0 / (latents.shape[0] * lax.axis_size(AXES))
    core = lax.axis_index("core").reshape(1)
    gain, bias = norm_gain[None], norm_bias[None]
    sel = jnp.asarray(SEL, jnp.bfloat16)
    held, got = gather_halves(conv_weight)
    keep, send = terms_of(core, latents, gain, bias, cotangent, sel)
    grad_weight = reduce_terms(keep, send) * scale
    output, grad_input = layer_of(core, latents, gain, bias, cotangent, held, got, sel)
    return (output, grad_input, grad_weight)


def solution(mesh):
    fine = Mesh(mesh.devices.reshape(4, 2, 8, 2, 8), AXES)
    batch = P(("xh", "core", "z", "xl", "y"), None, None, None)
    weight = P(None, ("z", "xl", "y"), None)
    return jax.shard_map(
        body,
        mesh=fine,
        in_specs=(batch, P(), P(), weight, batch),
        out_specs=(batch, batch, weight),
        check_vma=False,
    )
```

```python
import functools

import jax
import jax.numpy as jnp
import numpy as np
from jax import lax
from jax.experimental import pallas as pl
from jax.experimental.pallas import tpu as pltpu
from jax.sharding import Mesh
from jax.sharding import PartitionSpec as P

GROUPS = 32
HEIGHT, WIDTH, CHANS = 24, 20, 384
CELLS = HEIGHT * WIDTH
PER = CHANS // GROUPS
TOP = 32
ROWS = 9
YS, ZS = 8, 8
HIGH, LOW = 4, 2
SLOT = 28
QUAD = HIGH * SLOT
PACKED = (LOW * LOW, HIGH, QUAD, CHANS)
ZROWS = 2 * YS * ROWS
AXES = ("xh", "core", "zh", "zl", "xl", "yh", "yl")
SWAP = ((0, 0), (1, 2), (2, 1), (3, 3))
NEAR = ((1, 0), (2, 3), (3, 1), (0, 2))
TRADE = ((0, 1), (1, 0))
VMEM_LIMIT = 40 * 1024 * 1024


def placement():
    sel = np.zeros((2, LOW * QUAD, 3 * ZROWS), np.float32)
    for half in range(2):
        for y in range(YS):
            slot = (y % LOW) * QUAD + (y // LOW) * SLOT
            for i in range(3):
                for r in range(ROWS):
                    row = (half * YS + y) * ROWS + r
                    sel[half, slot + i * ROWS + r, i * ZROWS + row] = 1.0
    return sel


SEL = placement()


def dot(a, b, dims=((1,), (0,))):
    return lax.dot_general(a, b, (dims, ((), ())), preferred_element_type=jnp.float32)


def group_mean(row):
    a = lax.broadcasted_iota(jnp.int32, (CHANS, GROUPS), 0)
    b = lax.broadcasted_iota(jnp.int32, (CHANS, GROUPS), 1) * PER
    member = jnp.where((a >= b) & (a < b + PER), 1.0, 0.0).astype(jnp.float32)
    total = lax.dot_general(
        row, member, (((1,), (0,)), ((), ())),
        precision=lax.Precision.HIGHEST, preferred_element_type=jnp.float32,
    )
    back = lax.dot_general(
        total, member, (((1,), (1,)), ((), ())),
        precision=lax.Precision.HIGHEST, preferred_element_type=jnp.float32,
    )
    return back * (1.0 / (CELLS * PER))


def channel_sum(values):
    return jnp.broadcast_to(jnp.sum(values, axis=0, keepdims=True), (8, CHANS))


def statistics(flat):
    mean = group_mean(channel_sum(flat[...]))[0:1]
    centred = flat[...] - mean
    variance = group_mean(channel_sum(centred * centred))[0:1]
    return mean, 1.0 / jnp.sqrt(variance + 1e-05)


def build_patches(shifted, patches):
    row = lax.broadcasted_iota(jnp.int32, (CELLS, CHANS), 0) % HEIGHT
    for i in range(3):
        for j in range(3):
            start = TOP + (j - 1) * HEIGHT + (i - 1)
            tap = shifted[start : start + CELLS, :]
            if i == 0:
                tap = jnp.where(row == 0, 0.0, tap)
            if i == 2:
                tap = jnp.where(row == HEIGHT - 1, 0.0, tap)
            at = (i * 3 + j) * CHANS
            patches[:, at : at + CHANS] = tap.astype(jnp.bfloat16)


def clear_edges(shifted):
    edge = jnp.zeros((TOP, CHANS), jnp.float32)
    shifted[:TOP, :] = edge
    shifted[TOP + CELLS :, :] = edge


def activate(flat, gain, bias, shifted):
    mean, inverse = statistics(flat)
    normed = (flat[...] - mean) * inverse * gain[...] + bias[...]
    active = normed / (1.0 + jnp.exp(-normed))
    shifted[TOP : TOP + CELLS, :] = active.astype(jnp.bfloat16).astype(jnp.float32)
    return mean, inverse


def term_kernel(core, lat, gain, bias, cot, sel, keep, send, flat, shifted, patches, terms):
    clear_edges(shifted)
    flat[...] = lat[...].astype(jnp.float32)
    activate(flat, gain, bias, shifted)
    build_patches(shifted, patches)
    for t in range(9):
        at = t * CHANS
        terms[at : at + CHANS, :] = dot(patches[:, at : at + CHANS], cot[...], ((0,), (0,)))
    mine, other = sel[core[0]], sel[1 - core[0]]
    for z in range(ZS):
        block = jnp.concatenate(
            [terms[i * 3 * CHANS + z * ZROWS : i * 3 * CHANS + (z + 1) * ZROWS, :] for i in range(3)]
        )
        high = block.astype(jnp.bfloat16)
        low = (block - high.astype(jnp.float32)).astype(jnp.bfloat16)
        zh, zl = divmod(z, LOW)
        kept = dot(mine, high) + dot(mine, low)
        sent = dot(other, high).astype(jnp.bfloat16)
        for yl in range(LOW):
            keep[zl * LOW + yl, zh] = kept[yl * QUAD : (yl + 1) * QUAD]
            send[zl * LOW + yl, zh] = sent[yl * QUAD : (yl + 1) * QUAD]


def layer_kernel(
    core, lat, gain, bias, cot, held, got, sel, out, grad, flat, shifted, patches, weight
):
    clear_edges(shifted)
    flat[...] = lat[...].astype(jnp.float32)
    mean, inverse = activate(flat, gain, bias, shifted)
    build_patches(shifted, patches)
    mine, other = sel[core[0]], sel[1 - core[0]]
    for z in range(ZS):
        zh, zl = divmod(z, LOW)
        ours = jnp.concatenate([held[zl * LOW + yl, zh] for yl in range(LOW)])
        theirs = jnp.concatenate([got[zl * LOW + yl, zh] for yl in range(LOW)])
        block = dot(mine, ours, ((0,), (0,))) + dot(other, theirs, ((0,), (0,)))
        for i in range(3):
            at = i * 3 * CHANS + z * ZROWS
            weight[at : at + ZROWS, :] = block[i * ZROWS : (i + 1) * ZROWS].astype(jnp.bfloat16)
    out[...] = (dot(patches[...], weight[...]) + flat[...]).astype(jnp.bfloat16)
    shifted[TOP : TOP + CELLS, :] = cot[...].astype(jnp.float32)
    build_patches(shifted, patches)
    back = jnp.zeros((CELLS, CHANS), jnp.float32)
    for t in range(9):
        at, mirror = t * CHANS, (8 - t) * CHANS
        back = back + dot(
            patches[:, mirror : mirror + CHANS], weight[at : at + CHANS, :], ((1,), (1,))
        )
    hat = (flat[...] - mean) * inverse
    normed = hat * gain[...] + bias[...]
    gate = 1.0 / (1.0 + jnp.exp(-normed))
    back = back * (gate * (1.0 + normed * (1.0 - gate))) * gain[...]
    first = group_mean(channel_sum(back))[0:1]
    second = group_mean(channel_sum(back * hat))[0:1]
    result = cot[...].astype(jnp.float32) + inverse * (back - first - hat * second)
    grad[...] = result.astype(jnp.bfloat16)


VMEM = functools.partial(pl.BlockSpec, memory_space=pltpu.VMEM)
SMEM = functools.partial(pl.BlockSpec, memory_space=pltpu.SMEM)


def columns_first(maps):
    return maps.transpose(0, 2, 1, 3).reshape(CELLS, CHANS)


def rows_first(cells):
    return cells.reshape(1, WIDTH, HEIGHT, CHANS).transpose(0, 2, 1, 3)


def spread(block, axis):
    count = lax.axis_size(axis)
    copies = jnp.broadcast_to(block[None], (count,) + block.shape)
    return lax.all_to_all(copies, axis, 0, 0, tiled=True)


def gather_halves(conv_weight):
    taps, rows, chans = conv_weight.shape
    block = jnp.pad(conv_weight.reshape(taps * rows, chans), ((0, SLOT - taps * rows), (0, 0)))
    block = lax.ppermute(block, ("core", "xl"), SWAP)
    block = spread(block, ("zh", "yh")).reshape(PACKED[1:])
    held = spread(block, ("zl", "yl"))
    return held, lax.ppermute(held, "core", TRADE)


def halve_terms(keep, send):
    got = lax.ppermute(send, "core", TRADE)
    own = (keep + got.astype(jnp.float32)).astype(jnp.bfloat16)
    own = lax.all_to_all(own, ("zl", "yl"), 0, 0, tiled=True).astype(jnp.float32).sum(0)
    own = own.reshape(HIGH * HIGH, SLOT, CHANS).astype(jnp.bfloat16)
    return lax.all_to_all(own, ("zh", "yh"), 0, 0, tiled=True)


def finish_terms(parts):
    own = parts.astype(jnp.float32).sum(0)
    for bit in (1, 2):
        own = own + lax.ppermute(own, "xh", [(k, k ^ bit) for k in range(4)])
    pair = ("core", "xl")
    own = lax.ppermute(own, pair, NEAR) + lax.ppermute(own, pair, SWAP)
    return own[: 3 * ROWS].reshape(3, ROWS, CHANS)


def terms_of(core, latents, gain, bias, cotangent, sel, **options):
    return pl.pallas_call(
        term_kernel,
        out_shape=(
            jax.ShapeDtypeStruct(PACKED, jnp.float32),
            jax.ShapeDtypeStruct(PACKED, jnp.bfloat16),
        ),
        in_specs=[SMEM()] + [VMEM()] * 5,
        out_specs=(VMEM(), VMEM()),
        scratch_shapes=[
            pltpu.VMEM((CELLS, CHANS), jnp.float32),
            pltpu.VMEM((CELLS + 2 * TOP, CHANS), jnp.float32),
            pltpu.VMEM((CELLS, 9 * CHANS), jnp.bfloat16),
            pltpu.VMEM((9 * CHANS, CHANS), jnp.float32),
        ],
        compiler_params=pltpu.CompilerParams(vmem_limit_bytes=VMEM_LIMIT),
        cost_estimate=pl.CostEstimate(
            flops=4 * 10**9, bytes_accessed=8 * 10**6, transcendentals=CELLS * CHANS
        ),
        **options,
    )(core, latents, gain, bias, cotangent, sel)


def layer_of(core, latents, gain, bias, cotangent, held, got, sel, **options):
    return pl.pallas_call(
        layer_kernel,
        out_shape=(
            jax.ShapeDtypeStruct(latents.shape, jnp.bfloat16),
            jax.ShapeDtypeStruct(latents.shape, jnp.bfloat16),
        ),
        in_specs=[SMEM()] + [VMEM()] * 7,
        out_specs=(VMEM(), VMEM()),
        scratch_shapes=[
            pltpu.VMEM((CELLS, CHANS), jnp.float32),
            pltpu.VMEM((CELLS + 2 * TOP, CHANS), jnp.float32),
            pltpu.VMEM((CELLS, 9 * CHANS), jnp.bfloat16),
            pltpu.VMEM((9 * CHANS, CHANS), jnp.bfloat16),
        ],
        compiler_params=pltpu.CompilerParams(vmem_limit_bytes=VMEM_LIMIT),
        cost_estimate=pl.CostEstimate(
            flops=4 * 10**9, bytes_accessed=8 * 10**6, transcendentals=2 * CELLS * CHANS
        ),
        **options,
    )(core, latents, gain, bias, cotangent, held, got, sel)


def body(latents, norm_gain, norm_bias, conv_weight, cotangent):
    scale = 1.0 / (latents.shape[0] * lax.axis_size(AXES))
    core = lax.axis_index("core").reshape(1)
    gain, bias = norm_gain[None], norm_bias[None]
    sel = jnp.asarray(SEL, jnp.bfloat16)
    held, got = gather_halves(conv_weight)
    latents, cotangent = columns_first(latents), columns_first(cotangent)
    keep, send = terms_of(core, latents, gain, bias, cotangent, sel)
    parts = halve_terms(keep, send)
    output, grad_input = layer_of(core, latents, gain, bias, cotangent, held, got, sel)
    parts, output, grad_input = lax.optimization_barrier((parts, output, grad_input))
    grad_weight = finish_terms(parts) * scale
    return (rows_first(output), rows_first(grad_input), grad_weight)


def solution(mesh):
    fine = Mesh(mesh.devices.reshape(4, 2, HIGH, LOW, 2, HIGH, LOW), AXES)
    batch = P(AXES, None, None, None)
    weight = P(None, ("zh", "zl", "xl", "yh", "yl"), None)
    return jax.shard_map(
        body,
        mesh=fine,
        in_specs=(batch, P(), P(), weight, batch),
        out_specs=(batch, batch, weight),
        check_vma=False,
    )
```

```python
import functools

import jax
import jax.numpy as jnp
import numpy as np
from jax import lax
from jax.experimental import pallas as pl
from jax.experimental.pallas import tpu as pltpu
from jax.sharding import Mesh
from jax.sharding import PartitionSpec as P

GROUPS = 32
HEIGHT, WIDTH, CHANS = 24, 20, 384
CELLS = HEIGHT * WIDTH
PER = CHANS // GROUPS
TOP = 32
ROWS = 9
YS, ZS = 8, 8
HIGH, LOW = 4, 2
SLOT = 28
QUAD = HIGH * SLOT
PACKED = (LOW * LOW, HIGH, QUAD, CHANS)
ZROWS = 2 * YS * ROWS
AXES = ("xh", "core", "zh", "zl", "xl", "yh", "yl")
SWAP = ((0, 0), (1, 2), (2, 1), (3, 3))
NEAR = ((1, 0), (2, 3), (3, 1), (0, 2))
TRADE = ((0, 1), (1, 0))
VMEM_LIMIT = 40 * 1024 * 1024


def placement():
    sel = np.zeros((2, LOW * QUAD, 3 * ZROWS), np.float32)
    for half in range(2):
        for y in range(YS):
            slot = (y % LOW) * QUAD + (y // LOW) * SLOT
            for i in range(3):
                for r in range(ROWS):
                    row = (half * YS + y) * ROWS + r
                    sel[half, slot + i * ROWS + r, i * ZROWS + row] = 1.0
    return sel


SEL = placement()


def dot(a, b, dims=((1,), (0,))):
    return lax.dot_general(a, b, (dims, ((), ())), preferred_element_type=jnp.float32)


def group_mean(row):
    a = lax.broadcasted_iota(jnp.int32, (CHANS, GROUPS), 0)
    b = lax.broadcasted_iota(jnp.int32, (CHANS, GROUPS), 1) * PER
    member = jnp.where((a >= b) & (a < b + PER), 1.0, 0.0).astype(jnp.float32)
    total = lax.dot_general(
        row, member, (((1,), (0,)), ((), ())),
        precision=lax.Precision.HIGHEST, preferred_element_type=jnp.float32,
    )
    back = lax.dot_general(
        total, member, (((1,), (1,)), ((), ())),
        precision=lax.Precision.HIGHEST, preferred_element_type=jnp.float32,
    )
    return back * (1.0 / (CELLS * PER))


def channel_sum(values):
    return jnp.broadcast_to(jnp.sum(values, axis=0, keepdims=True), (8, CHANS))


def statistics(flat):
    mean = group_mean(channel_sum(flat[...]))[0:1]
    centred = flat[...] - mean
    variance = group_mean(channel_sum(centred * centred))[0:1]
    return mean, 1.0 / jnp.sqrt(variance + 1e-05)


def build_patches(shifted, patches):
    row = lax.broadcasted_iota(jnp.int32, (CELLS, CHANS), 0) % HEIGHT
    for i in range(3):
        for j in range(3):
            start = TOP + (j - 1) * HEIGHT + (i - 1)
            tap = shifted[start : start + CELLS, :]
            if i == 0:
                tap = jnp.where(row == 0, 0.0, tap)
            if i == 2:
                tap = jnp.where(row == HEIGHT - 1, 0.0, tap)
            at = (i * 3 + j) * CHANS
            patches[:, at : at + CHANS] = tap.astype(jnp.bfloat16)


def clear_edges(shifted):
    edge = jnp.zeros((TOP, CHANS), jnp.float32)
    shifted[:TOP, :] = edge
    shifted[TOP + CELLS :, :] = edge


def activate(flat, gain, bias, shifted):
    mean, inverse = statistics(flat)
    normed = (flat[...] - mean) * inverse * gain[...] + bias[...]
    active = normed / (1.0 + jnp.exp(-normed))
    shifted[TOP : TOP + CELLS, :] = active.astype(jnp.bfloat16).astype(jnp.float32)
    return mean, inverse


def term_kernel(here, lat, gain, bias, cot, sel, keep, send, flat, shifted, patches, terms):
    clear_edges(shifted)
    flat[...] = lat[...].astype(jnp.float32)
    activate(flat, gain, bias, shifted)
    build_patches(shifted, patches)
    for t in range(9):
        at = t * CHANS
        terms[at : at + CHANS, :] = dot(patches[:, at : at + CHANS], cot[...], ((0,), (0,)))
    mine, other = sel[here[0]], sel[1 - here[0]]
    for z in range(ZS):
        block = jnp.concatenate(
            [terms[i * 3 * CHANS + z * ZROWS : i * 3 * CHANS + (z + 1) * ZROWS, :] for i in range(3)]
        )
        high = block.astype(jnp.bfloat16)
        low = (block - high.astype(jnp.float32)).astype(jnp.bfloat16)
        zh, zl = divmod(z, LOW)
        kept = dot(mine, high) + dot(mine, low)
        sent = dot(other, high).astype(jnp.bfloat16)
        for yl in range(LOW):
            keep[zl * LOW + yl, zh] = kept[yl * QUAD : (yl + 1) * QUAD]
            send[zl * LOW + yl, zh] = sent[yl * QUAD : (yl + 1) * QUAD]


def layer_kernel(
    here, lat, gain, bias, cot, held, got, sel, out, grad, flat, shifted, patches, weight
):
    clear_edges(shifted)
    flat[...] = lat[...].astype(jnp.float32)
    mean, inverse = activate(flat, gain, bias, shifted)
    build_patches(shifted, patches)
    mine, other = sel[here[0]], sel[1 - here[0]]
    for z in range(ZS):
        zh, zl = divmod(z, LOW)
        ahead = lax.rem(zh + HIGH - here[1], HIGH)
        flips = [(zl ^ here[2]) * LOW + (yl ^ here[3]) for yl in range(LOW)]
        ours = jnp.concatenate([held[flip, ahead] for flip in flips])
        theirs = jnp.concatenate([got[flip, ahead] for flip in flips])
        block = dot(mine, ours, ((0,), (0,))) + dot(other, theirs, ((0,), (0,)))
        for i in range(3):
            at = i * 3 * CHANS + z * ZROWS
            weight[at : at + ZROWS, :] = block[i * ZROWS : (i + 1) * ZROWS].astype(jnp.bfloat16)
    out[...] = (dot(patches[...], weight[...]) + flat[...]).astype(jnp.bfloat16)
    shifted[TOP : TOP + CELLS, :] = cot[...].astype(jnp.float32)
    build_patches(shifted, patches)
    back = jnp.zeros((CELLS, CHANS), jnp.float32)
    for t in range(9):
        at, mirror = t * CHANS, (8 - t) * CHANS
        back = back + dot(
            patches[:, mirror : mirror + CHANS], weight[at : at + CHANS, :], ((1,), (1,))
        )
    hat = (flat[...] - mean) * inverse
    normed = hat * gain[...] + bias[...]
    gate = 1.0 / (1.0 + jnp.exp(-normed))
    back = back * (gate * (1.0 + normed * (1.0 - gate))) * gain[...]
    first = group_mean(channel_sum(back))[0:1]
    second = group_mean(channel_sum(back * hat))[0:1]
    result = cot[...].astype(jnp.float32) + inverse * (back - first - hat * second)
    grad[...] = result.astype(jnp.bfloat16)


VMEM = functools.partial(pl.BlockSpec, memory_space=pltpu.VMEM)
SMEM = functools.partial(pl.BlockSpec, memory_space=pltpu.SMEM)


def columns_first(maps):
    return maps.transpose(0, 2, 1, 3).reshape(CELLS, CHANS)


def rows_first(cells):
    return cells.reshape(1, WIDTH, HEIGHT, CHANS).transpose(0, 2, 1, 3)


def gather_slots(conv_weight):
    taps, rows, chans = conv_weight.shape
    block = jnp.pad(conv_weight.reshape(taps * rows, chans), ((0, SLOT - taps * rows), (0, 0)))
    slots = [lax.ppermute(block, ("core", "xl", "yh"), from_ahead(j)) for j in range(HIGH)]
    ahead = lax.rem(HIGH - lax.axis_index("yh"), HIGH)
    return lax.dynamic_slice_in_dim(jnp.stack(slots + slots[:-1]), ahead, HIGH).reshape(QUAD, chans)


def gather_half(block):
    ring = range(HIGH)
    steps = [[((k + j) % HIGH, k) for k in ring] for j in ring[1:]]
    block = jnp.stack([block] + [lax.ppermute(block, "zh", step) for step in steps])
    flips = [[(k ^ bits, k) for k in range(4)] for bits in (1, 2, 3)]
    return jnp.stack([block] + [lax.ppermute(block, ("zl", "yl"), flip) for flip in flips])


def from_ahead(j):
    return [
        ((x * 2 + c) * HIGH + (y + j) % HIGH, (c * 2 + x) * HIGH + y)
        for c in range(2)
        for y in range(HIGH)
        for x in range(2)
    ]


def add_cores(keep, send):
    got = lax.ppermute(send, "core", TRADE)
    return (keep + got.astype(jnp.float32)).astype(jnp.bfloat16)


def add_neighbours(own):
    own = lax.all_to_all(own, ("zl", "yl"), 0, 0, tiled=True).astype(jnp.float32).sum(0)
    return own.reshape(HIGH * HIGH, SLOT, CHANS).astype(jnp.bfloat16)


def finish_terms(parts):
    own = parts.astype(jnp.float32).sum(0)
    near, far, both = [
        lax.ppermute(own, "xh", [(k, k ^ bits) for k in range(4)]) for bits in (1, 2, 3)
    ]
    own = (own + far) + (near + both)
    pair = ("core", "xl")
    own = lax.ppermute(own, pair, NEAR) + lax.ppermute(own, pair, SWAP)
    return own[: 3 * ROWS].reshape(3, ROWS, CHANS)


def terms_of(here, latents, gain, bias, cotangent, sel, **options):
    return pl.pallas_call(
        term_kernel,
        out_shape=(
            jax.ShapeDtypeStruct(PACKED, jnp.float32),
            jax.ShapeDtypeStruct(PACKED, jnp.bfloat16),
        ),
        in_specs=[SMEM()] + [VMEM()] * 5,
        out_specs=(VMEM(), VMEM()),
        scratch_shapes=[
            pltpu.VMEM((CELLS, CHANS), jnp.float32),
            pltpu.VMEM((CELLS + 2 * TOP, CHANS), jnp.float32),
            pltpu.VMEM((CELLS, 9 * CHANS), jnp.bfloat16),
            pltpu.VMEM((9 * CHANS, CHANS), jnp.float32),
        ],
        compiler_params=pltpu.CompilerParams(vmem_limit_bytes=VMEM_LIMIT),
        cost_estimate=pl.CostEstimate(
            flops=4 * 10**9, bytes_accessed=8 * 10**6, transcendentals=CELLS * CHANS
        ),
        **options,
    )(here, latents, gain, bias, cotangent, sel)


def layer_of(here, latents, gain, bias, cotangent, held, got, sel, **options):
    return pl.pallas_call(
        layer_kernel,
        out_shape=(
            jax.ShapeDtypeStruct(latents.shape, jnp.bfloat16),
            jax.ShapeDtypeStruct(latents.shape, jnp.bfloat16),
        ),
        in_specs=[SMEM()] + [VMEM()] * 7,
        out_specs=(VMEM(), VMEM()),
        scratch_shapes=[
            pltpu.VMEM((CELLS, CHANS), jnp.float32),
            pltpu.VMEM((CELLS + 2 * TOP, CHANS), jnp.float32),
            pltpu.VMEM((CELLS, 9 * CHANS), jnp.bfloat16),
            pltpu.VMEM((9 * CHANS, CHANS), jnp.bfloat16),
        ],
        compiler_params=pltpu.CompilerParams(vmem_limit_bytes=VMEM_LIMIT),
        cost_estimate=pl.CostEstimate(
            flops=4 * 10**9, bytes_accessed=8 * 10**6, transcendentals=2 * CELLS * CHANS
        ),
        **options,
    )(here, latents, gain, bias, cotangent, held, got, sel)


def body(latents, norm_gain, norm_bias, conv_weight, cotangent):
    scale = 1.0 / (latents.shape[0] * lax.axis_size(AXES))
    here = jnp.stack([lax.axis_index(axis) for axis in ("core", "zh", "zl", "yl")])
    gain, bias = norm_gain[None], norm_bias[None]
    sel = jnp.asarray(SEL, jnp.bfloat16)
    latents, cotangent = columns_first(latents), columns_first(cotangent)
    keep, send = terms_of(here, latents, gain, bias, cotangent, sel)
    keep, send, conv_weight = lax.optimization_barrier((keep, send, conv_weight))
    own, block = lax.optimization_barrier((add_cores(keep, send), gather_slots(conv_weight)))
    own, held = lax.optimization_barrier((add_neighbours(own), gather_half(block)))
    parts = lax.all_to_all(own, ("zh", "yh"), 0, 0, tiled=True)
    got = lax.ppermute(held, "core", TRADE)
    output, grad_input = layer_of(here, latents, gain, bias, cotangent, held, got, sel)
    parts, output, grad_input = lax.optimization_barrier((parts, output, grad_input))
    grad_weight = finish_terms(parts) * scale
    return (rows_first(output), rows_first(grad_input), grad_weight)


def solution(mesh):
    fine = Mesh(mesh.devices.reshape(4, 2, HIGH, LOW, 2, HIGH, LOW), AXES)
    batch = P(AXES, None, None, None)
    weight = P(None, ("zh", "zl", "xl", "yh", "yl"), None)
    return jax.shard_map(
        body,
        mesh=fine,
        in_specs=(batch, P(), P(), weight, batch),
        out_specs=(batch, batch, weight),
        check_vma=False,
    )
```

```python
import functools

import jax
import jax.numpy as jnp
import numpy as np
from jax import lax
from jax.experimental import pallas as pl
from jax.experimental.pallas import tpu as pltpu
from jax.sharding import Mesh
from jax.sharding import PartitionSpec as P

GROUPS = 32
HEIGHT, WIDTH, CHANS = 24, 20, 384
CELLS = HEIGHT * WIDTH
PER = CHANS // GROUPS
TOP = 32
ROWS = 9
YS, ZS = 8, 8
HIGH, LOW = 4, 2
SLOT = 28
QUAD = HIGH * SLOT
PACKED = (LOW * LOW, HIGH, QUAD, CHANS)
ZROWS = 2 * YS * ROWS
AXES = ("xh", "core", "zh", "zl", "xl", "yh", "yl")
SWAP = ((0, 0), (1, 2), (2, 1), (3, 3))
NEAR = ((1, 0), (2, 3), (3, 1), (0, 2))
TRADE = ((0, 1), (1, 0))
VMEM_LIMIT = 40 * 1024 * 1024


def placement():
    sel = np.zeros((2, LOW * QUAD, 3 * ZROWS), np.float32)
    for half in range(2):
        for y in range(YS):
            slot = (y % LOW) * QUAD + (y // LOW) * SLOT
            for i in range(3):
                for r in range(ROWS):
                    row = (half * YS + y) * ROWS + r
                    sel[half, slot + i * ROWS + r, i * ZROWS + row] = 1.0
    return sel


SEL = placement()


def dot(a, b, dims=((1,), (0,))):
    return lax.dot_general(a, b, (dims, ((), ())), preferred_element_type=jnp.float32)


def group_mean(row):
    a = lax.broadcasted_iota(jnp.int32, (CHANS, GROUPS), 0)
    b = lax.broadcasted_iota(jnp.int32, (CHANS, GROUPS), 1) * PER
    member = jnp.where((a >= b) & (a < b + PER), 1.0, 0.0).astype(jnp.float32)
    total = lax.dot_general(
        row, member, (((1,), (0,)), ((), ())),
        precision=lax.Precision.HIGHEST, preferred_element_type=jnp.float32,
    )
    back = lax.dot_general(
        total, member, (((1,), (1,)), ((), ())),
        precision=lax.Precision.HIGHEST, preferred_element_type=jnp.float32,
    )
    return back * (1.0 / (CELLS * PER))


def channel_sum(values):
    return jnp.broadcast_to(jnp.sum(values, axis=0, keepdims=True), (8, CHANS))


def statistics(flat):
    mean = group_mean(channel_sum(flat[...]))[0:1]
    centred = flat[...] - mean
    variance = group_mean(channel_sum(centred * centred))[0:1]
    return mean, 1.0 / jnp.sqrt(variance + 1e-05)


def build_patches(shifted, patches):
    row = lax.broadcasted_iota(jnp.int32, (CELLS, CHANS), 0) % HEIGHT
    for i in range(3):
        for j in range(3):
            start = TOP + (j - 1) * HEIGHT + (i - 1)
            tap = shifted[start : start + CELLS, :]
            if i == 0:
                tap = jnp.where(row == 0, 0.0, tap)
            if i == 2:
                tap = jnp.where(row == HEIGHT - 1, 0.0, tap)
            at = (i * 3 + j) * CHANS
            patches[:, at : at + CHANS] = tap.astype(jnp.bfloat16)


def clear_edges(shifted):
    edge = jnp.zeros((TOP, CHANS), jnp.float32)
    shifted[:TOP, :] = edge
    shifted[TOP + CELLS :, :] = edge


def activate(flat, gain, bias, shifted):
    mean, inverse = statistics(flat)
    normed = (flat[...] - mean) * inverse * gain[...] + bias[...]
    active = normed / (1.0 + jnp.exp(-normed))
    shifted[TOP : TOP + CELLS, :] = active.astype(jnp.bfloat16).astype(jnp.float32)
    return mean, inverse


def term_kernel(core, lat, gain, bias, cot, sel, keep, send, flat, shifted, patches, terms):
    clear_edges(shifted)
    flat[...] = lat[...].astype(jnp.float32)
    activate(flat, gain, bias, shifted)
    build_patches(shifted, patches)
    for t in range(9):
        at = t * CHANS
        terms[at : at + CHANS, :] = dot(patches[:, at : at + CHANS], cot[...], ((0,), (0,)))
    mine, other = sel[core[0]], sel[1 - core[0]]
    for z in range(ZS):
        block = jnp.concatenate(
            [terms[i * 3 * CHANS + z * ZROWS : i * 3 * CHANS + (z + 1) * ZROWS, :] for i in range(3)]
        )
        high = block.astype(jnp.bfloat16)
        low = (block - high.astype(jnp.float32)).astype(jnp.bfloat16)
        zh, zl = divmod(z, LOW)
        kept = dot(mine, high) + dot(mine, low)
        sent = dot(other, high).astype(jnp.bfloat16)
        for yl in range(LOW):
            keep[zl * LOW + yl, zh] = kept[yl * QUAD : (yl + 1) * QUAD]
            send[zl * LOW + yl, zh] = sent[yl * QUAD : (yl + 1) * QUAD]


def layer_kernel(
    core, lat, gain, bias, cot, held, got, sel, out, grad, flat, shifted, patches, weight
):
    clear_edges(shifted)
    flat[...] = lat[...].astype(jnp.float32)
    mean, inverse = activate(flat, gain, bias, shifted)
    build_patches(shifted, patches)
    mine, other = sel[core[0]], sel[1 - core[0]]
    for z in range(ZS):
        zh, zl = divmod(z, LOW)
        ours = jnp.concatenate([held[zl * LOW + yl, zh] for yl in range(LOW)])
        theirs = jnp.concatenate([got[zl * LOW + yl, zh] for yl in range(LOW)])
        block = dot(mine, ours, ((0,), (0,))) + dot(other, theirs, ((0,), (0,)))
        for i in range(3):
            at = i * 3 * CHANS + z * ZROWS
            weight[at : at + ZROWS, :] = block[i * ZROWS : (i + 1) * ZROWS].astype(jnp.bfloat16)
    out[...] = (dot(patches[...], weight[...]) + flat[...]).astype(jnp.bfloat16)
    shifted[TOP : TOP + CELLS, :] = cot[...].astype(jnp.float32)
    build_patches(shifted, patches)
    back = jnp.zeros((CELLS, CHANS), jnp.float32)
    for t in range(9):
        at, mirror = t * CHANS, (8 - t) * CHANS
        back = back + dot(
            patches[:, mirror : mirror + CHANS], weight[at : at + CHANS, :], ((1,), (1,))
        )
    hat = (flat[...] - mean) * inverse
    normed = hat * gain[...] + bias[...]
    gate = 1.0 / (1.0 + jnp.exp(-normed))
    back = back * (gate * (1.0 + normed * (1.0 - gate))) * gain[...]
    first = group_mean(channel_sum(back))[0:1]
    second = group_mean(channel_sum(back * hat))[0:1]
    result = cot[...].astype(jnp.float32) + inverse * (back - first - hat * second)
    grad[...] = result.astype(jnp.bfloat16)


VMEM = functools.partial(pl.BlockSpec, memory_space=pltpu.VMEM)
SMEM = functools.partial(pl.BlockSpec, memory_space=pltpu.SMEM)


def columns_first(maps):
    return maps.transpose(0, 2, 1, 3).reshape(CELLS, CHANS)


def rows_first(cells):
    return cells.reshape(1, WIDTH, HEIGHT, CHANS).transpose(0, 2, 1, 3)


def spread(block, axis):
    count = lax.axis_size(axis)
    copies = jnp.broadcast_to(block[None], (count,) + block.shape)
    return lax.all_to_all(copies, axis, 0, 0, tiled=True)


def gather_slots(conv_weight):
    taps, rows, chans = conv_weight.shape
    block = jnp.pad(conv_weight.reshape(taps * rows, chans), ((0, SLOT - taps * rows), (0, 0)))
    block = lax.ppermute(block, ("core", "xl"), SWAP)
    return lax.all_gather(block, ("zh", "yh")).reshape(PACKED[1:])


def halve_terms(keep, send):
    got = lax.ppermute(send, "core", TRADE)
    own = (keep + got.astype(jnp.float32)).astype(jnp.bfloat16)
    own = lax.all_to_all(own, ("zl", "yl"), 0, 0, tiled=True).astype(jnp.float32).sum(0)
    own = own.reshape(HIGH * HIGH, SLOT, CHANS).astype(jnp.bfloat16)
    return lax.all_to_all(own, ("zh", "yh"), 0, 0, tiled=True)


def finish_terms(parts):
    own = parts.astype(jnp.float32).sum(0)
    for bit in (1, 2):
        own = own + lax.ppermute(own, "xh", [(k, k ^ bit) for k in range(4)])
    pair = ("core", "xl")
    own = lax.ppermute(own, pair, NEAR) + lax.ppermute(own, pair, SWAP)
    return own[: 3 * ROWS].reshape(3, ROWS, CHANS)


def terms_of(core, latents, gain, bias, cotangent, sel, **options):
    return pl.pallas_call(
        term_kernel,
        out_shape=(
            jax.ShapeDtypeStruct(PACKED, jnp.float32),
            jax.ShapeDtypeStruct(PACKED, jnp.bfloat16),
        ),
        in_specs=[SMEM()] + [VMEM()] * 5,
        out_specs=(VMEM(), VMEM()),
        scratch_shapes=[
            pltpu.VMEM((CELLS, CHANS), jnp.float32),
            pltpu.VMEM((CELLS + 2 * TOP, CHANS), jnp.float32),
            pltpu.VMEM((CELLS, 9 * CHANS), jnp.bfloat16),
            pltpu.VMEM((9 * CHANS, CHANS), jnp.float32),
        ],
        compiler_params=pltpu.CompilerParams(vmem_limit_bytes=VMEM_LIMIT),
        cost_estimate=pl.CostEstimate(
            flops=4 * 10**9, bytes_accessed=8 * 10**6, transcendentals=CELLS * CHANS
        ),
        **options,
    )(core, latents, gain, bias, cotangent, sel)


def layer_of(core, latents, gain, bias, cotangent, held, got, sel, **options):
    return pl.pallas_call(
        layer_kernel,
        out_shape=(
            jax.ShapeDtypeStruct(latents.shape, jnp.bfloat16),
            jax.ShapeDtypeStruct(latents.shape, jnp.bfloat16),
        ),
        in_specs=[SMEM()] + [VMEM()] * 7,
        out_specs=(VMEM(), VMEM()),
        scratch_shapes=[
            pltpu.VMEM((CELLS, CHANS), jnp.float32),
            pltpu.VMEM((CELLS + 2 * TOP, CHANS), jnp.float32),
            pltpu.VMEM((CELLS, 9 * CHANS), jnp.bfloat16),
            pltpu.VMEM((9 * CHANS, CHANS), jnp.bfloat16),
        ],
        compiler_params=pltpu.CompilerParams(vmem_limit_bytes=VMEM_LIMIT),
        cost_estimate=pl.CostEstimate(
            flops=4 * 10**9, bytes_accessed=8 * 10**6, transcendentals=2 * CELLS * CHANS
        ),
        **options,
    )(core, latents, gain, bias, cotangent, held, got, sel)


def body(latents, norm_gain, norm_bias, conv_weight, cotangent):
    scale = 1.0 / (latents.shape[0] * lax.axis_size(AXES))
    core = lax.axis_index("core").reshape(1)
    gain, bias = norm_gain[None], norm_bias[None]
    sel = jnp.asarray(SEL, jnp.bfloat16)
    block = gather_slots(conv_weight)
    latents, cotangent = columns_first(latents), columns_first(cotangent)
    keep, send = terms_of(core, latents, gain, bias, cotangent, sel)
    parts = halve_terms(keep, send)
    parts, block = lax.optimization_barrier((parts, block))
    held = spread(block, ("zl", "yl"))
    got = lax.ppermute(held, "core", TRADE)
    grad_weight = finish_terms(parts) * scale
    output, grad_input = layer_of(core, latents, gain, bias, cotangent, held, got, sel)
    return (rows_first(output), rows_first(grad_input), grad_weight)


def solution(mesh):
    fine = Mesh(mesh.devices.reshape(4, 2, HIGH, LOW, 2, HIGH, LOW), AXES)
    batch = P(AXES, None, None, None)
    weight = P(None, ("zh", "zl", "xl", "yh", "yl"), None)
    return jax.shard_map(
        body,
        mesh=fine,
        in_specs=(batch, P(), P(), weight, batch),
        out_specs=(batch, batch, weight),
        check_vma=False,
    )
```
